32 devices in a mesh: dp: 8 (over z, y), feat: 4 (over x, core).
Axes of the slice: x: 2, y: 2, z: 4, core: 2. Of those that a mesh axis runs over, the one named last changes fastest.
Arguments:
- activations: bfloat16 [8192, 8192], P('dp', 'feat'), may hold values from -6 to 6
- cand_index: int32 [8192], P('dp'), may hold values from 0 to 7
- labels: int32 [512], P('dp'), may hold values 0 or 1
- counts: int32 [8], P('dp'), may hold values from 1 to 64, as said below
Outputs:
- scores: float32 [8192, 8], P('dp', 'feat')
The draws below stay inside these ranges and needn't reach their ends.
Inputs may be any that keep to these rules, and one draw needn't show every extreme that they name: `counts`: the fullest slab has all 64 prompt slots live.
All inputs are finite; a program needn't handle non-finite values. No bound on the sum of `labels` on one device may be relied on, other than what follows from the above.
Results may differ from the reference program's by a relative error of at most 0.0047.
Values may be sent and summed in bfloat16 or wider, within the bound.
No kernel may reach another device: no remote copies, remote signals or barrier semaphores. Data moves between devices by JAX's collectives and lax.ppermute only.
A program may use at most 64 MiB of HBM per device.

```python
import jax
import jax.numpy as jnp
from jax import lax

D = 8192
PER_PROMPT = 16
ROW_DEV = 1024
PROMPT_DEV = 64
SLABS = 8
CANDS = 8
ROWS = 8192
PROMPTS = 512


def draw_counts(key, part):
    lowest = max(1, PROMPT_DEV // 4)
    values = jax.random.randint(key, (SLABS,), lowest, PROMPT_DEV + 1)
    chosen_slab = jax.random.randint(jax.random.fold_in(key, 7), (), 0, SLABS)
    return values.at[chosen_slab].set(PROMPT_DEV).astype(jnp.int32)


def touch_ends(values, key, low, top_value):
    index_at = [jax.random.randint(jax.random.fold_in(key, axis), (), 0, length) for axis, length in enumerate(values.shape)]
    longest = values.shape.index(max(values.shape))
    beside = index_at[:longest] + [(index_at[longest] + 1) % values.shape[longest]] + index_at[longest + 1:]
    return values.at[tuple(index_at)].set(low).at[tuple(beside)].set(top_value)


def level_of(key, dims, cuts, least, top_value):
    level = 1.0
    for position, shards_of in cuts:
        heights = jax.random.uniform(jax.random.fold_in(jax.random.fold_in(key, 6), position), (shards_of,), jnp.float32, least / len(cuts), top_value / len(cuts))
        level = level * jnp.repeat(jnp.exp(heights), dims[position] // shards_of).reshape((-1,) + (1,) * (len(dims) - 1 - position))
    return level


def scatter_about(rng, dims, width, limit, split=(), kind=jnp.bfloat16):
    array = width * jax.random.normal(rng, dims, jnp.float32)
    if split:
        array = array * level_of(rng, dims, split, -0.22, 0.18)
    return jnp.clip(array, -limit, limit).astype(kind)


def setup_inputs(seed: int = 0) -> dict:
    arg_keys = jax.random.split(jax.random.key(seed), 5)
    return {
        "activations": scatter_about(arg_keys[0], (ROWS, D), 1.0, 6.0, ((0, 8), (1, 4))),
        "cand_index": touch_ends(jax.random.randint(arg_keys[1], (ROWS,), 0, CANDS), jax.random.fold_in(arg_keys[1], 1), 0, CANDS - 1).astype(jnp.int32),
        "labels": touch_ends((jax.random.randint(arg_keys[2], (PROMPTS,), 0, 2) < 1).astype(jnp.int32), jax.random.fold_in(arg_keys[2], 1), 0, 1),
        "counts": draw_counts(jax.random.fold_in(arg_keys[4], 71), 0),
    }


epsilon = 1e-06

def reference(activations, cand_index, labels, counts):
    row_total = activations.shape[0]
    row_ids = jnp.arange(row_total, dtype=jnp.int32)
    slab_of = row_ids // ROW_DEV
    prompt_of = row_ids // PER_PROMPT
    live = prompt_of % PROMPT_DEV < counts[slab_of]
    classes = labels[prompt_of]
    cand_ids = jnp.arange(CANDS, dtype=jnp.int32)
    matches = (cand_index[None, :] == cand_ids[:, None]) & live[None, :]
    harmful_hits = matches & (classes[None, :] == 1)
    harmless_hits = matches & (classes[None, :] == 0)
    member = jnp.concatenate([harmful_hits, harmless_hits], axis=0).astype(jnp.bfloat16)
    class_sums = jnp.dot(member, activations, preferred_element_type=jnp.float32)
    class_counts = lax.optimization_barrier(jnp.sum(member.astype(jnp.float32), axis=1))
    harmful_mean = class_sums[:CANDS] / jnp.maximum(class_counts[:CANDS], 1.0)[:, None]
    harmless_mean = class_sums[CANDS:] / jnp.maximum(class_counts[CANDS:], 1.0)[:, None]
    raw_dir = (harmful_mean - harmless_mean).astype(jnp.bfloat16)
    squares = lax.optimization_barrier(jnp.sum(jnp.square(raw_dir.astype(jnp.float32)), axis=1))
    inv_norm = lax.rsqrt(squares + epsilon).astype(jnp.bfloat16)
    plain = jnp.dot(activations, raw_dir.T, preferred_element_type=jnp.float32)
    return plain * inv_norm.astype(jnp.float32)[None, :]
```

```python
import functools

import jax
import jax.numpy as jnp
from jax import lax
from jax.experimental import pallas as pl
from jax.experimental.pallas import tpu as pltpu
from jax.sharding import PartitionSpec as P

CAND_DEV = 1
PER_PROMPT = 16
LANES = 128
VMEM_LIMIT = 32 * 1024 * 1024

epsilon = 1e-06


def sums_kernel(steps, counts_ref, cand_ref, labels_ref, acts_hbm, sums_ref, acts_ref, sems):
    rows, width = acts_ref.shape
    classes = sums_ref.shape[0]
    cands = classes // 2
    prompts = labels_ref.shape[1]
    tall = rows // steps

    def fetch(step):
        part = pl.ds(step * tall, tall)
        return pltpu.make_async_copy(acts_hbm.at[part, :], acts_ref.at[part, :], sems.at[step])

    for step in range(steps):
        fetch(step).start()

    prompt_ids = lax.broadcasted_iota(jnp.int32, (prompts, rows), 0)
    prompt_of = lax.broadcasted_iota(jnp.int32, (prompts, rows), 1) // PER_PROMPT
    spread = jnp.where(prompt_ids == prompt_of, 1.0, 0.0).astype(jnp.bfloat16)
    labels = jnp.broadcast_to(labels_ref[...].astype(jnp.float32), (8, prompts))
    row_class = jnp.dot(labels.astype(jnp.bfloat16), spread, preferred_element_type=jnp.float32)[:1]
    live = lax.broadcasted_iota(jnp.int32, (1, rows), 1) // PER_PROMPT < counts_ref[0]
    wanted = lax.broadcasted_iota(jnp.int32, (classes, rows), 0)
    slot = jnp.where(row_class == 1.0, cand_ref[...], cand_ref[...] + cands)
    slot = jnp.where(live, slot, -1)
    member_float = jnp.where(wanted == slot, 1.0, 0.0)
    member = member_float.astype(jnp.bfloat16)
    tally = jnp.sum(member_float, axis=1, keepdims=True)
    sums_ref[:, width:] = jnp.broadcast_to(tally, (classes, LANES))

    total = None
    for step in range(steps):
        fetch(step).wait()
        piece = jnp.dot(
            member[:, step * tall : (step + 1) * tall],
            acts_ref[step * tall : (step + 1) * tall, :],
            preferred_element_type=jnp.float32,
        )
        total = piece if total is None else total + piece
    sums_ref[:, :width] = total


def class_sums(activations, cand_index, labels, counts, classes, steps=8):
    rows, width = activations.shape
    vmem = pl.BlockSpec(memory_space=pltpu.VMEM)
    return pl.pallas_call(
        functools.partial(sums_kernel, steps),
        out_shape=(
            jax.ShapeDtypeStruct((classes, width + LANES), jnp.float32),
            pltpu.VMEM((rows, width), activations.dtype),
        ),
        in_specs=[
            pl.BlockSpec(memory_space=pltpu.SMEM),
            vmem,
            vmem,
            pl.BlockSpec(memory_space=pltpu.HBM),
        ],
        out_specs=(vmem, vmem),
        scratch_shapes=[pltpu.SemaphoreType.DMA((steps,))],
        compiler_params=pltpu.CompilerParams(vmem_limit_bytes=VMEM_LIMIT),
        name="class_sums",
    )(counts, cand_index.reshape(1, rows), labels.reshape(1, -1), pltpu.with_memory_space_constraint(activations, pltpu.HBM))


def project_kernel(upper_ref, mine_ref, other_ref, acts_ref, keep_ref, send_ref):
    rows, width = acts_ref.shape
    cands = mine_ref.shape[0] // 2
    half = cands // 2
    total = mine_ref[...] + other_ref[...]
    tally = jnp.maximum(total[:, width : width + 1], 1.0)
    harmful_mean = total[:cands, :width] / tally[:cands]
    harmless_mean = total[cands:, :width] / tally[cands:]
    raw_dir = (harmful_mean - harmless_mean).astype(jnp.bfloat16)
    squares = jnp.sum(jnp.square(raw_dir.astype(jnp.float32)), axis=1, keepdims=True)
    squares = jnp.broadcast_to(squares, (cands, LANES))
    plain = lax.dot_general(
        raw_dir, acts_ref[...], (((1,), (1,)), ((), ())), preferred_element_type=jnp.float32
    )
    upper = upper_ref[0] == 1
    keep_ref[:, :rows] = jnp.where(upper, plain[half:], plain[:half])
    send_ref[:, :rows] = jnp.where(upper, plain[:half], plain[half:])
    keep_ref[:, rows:] = jnp.where(upper, squares[half:], squares[:half])
    send_ref[:, rows:] = jnp.where(upper, squares[:half], squares[half:])


def project(upper, mine, other, acts):
    rows = acts.shape[0]
    cands = mine.shape[0] // 2
    vmem = pl.BlockSpec(memory_space=pltpu.VMEM)
    half = jax.ShapeDtypeStruct((cands // 2, rows + LANES), jnp.float32)
    return pl.pallas_call(
        project_kernel,
        out_shape=(half, half),
        in_specs=[pl.BlockSpec(memory_space=pltpu.SMEM), vmem, vmem, vmem],
        out_specs=(vmem, vmem),
        compiler_params=pltpu.CompilerParams(vmem_limit_bytes=VMEM_LIMIT),
        name="project",
    )(upper, mine, other, pltpu.with_memory_space_constraint(acts, pltpu.VMEM))


def trade(value, axis, bit):
    return lax.ppermute(value, axis, [(i, i ^ bit) for i in range(lax.axis_size(axis))])


def per_device(activations, cand_index, labels, counts):
    rows = activations.shape[0]
    dp, feat = lax.axis_size("dp"), lax.axis_size("feat")
    cands = CAND_DEV * dp
    sums, acts = class_sums(activations, cand_index, labels, counts, 2 * cands)

    bit = 1
    while 2 * bit < dp:
        sums = sums + trade(sums, "dp", bit)
        bit *= 2
    other = trade(sums, "dp", bit)

    place = lax.axis_index("feat")
    bit = feat // 2
    upper = (place // bit % 2).astype(jnp.int32).reshape(1)
    keep, send = project(upper, sums, other, acts)
    keep = keep + trade(send, "feat", bit)
    while bit > 1:
        bit //= 2
        half = keep.shape[0] // 2
        upper = place // bit % 2 == 1
        low, high = keep[:half], keep[half:]
        keep = jnp.where(upper, high, low) + trade(jnp.where(upper, low, high), "feat", bit)
    inv_norm = lax.rsqrt(keep[:, rows : rows + 1] + epsilon).astype(jnp.bfloat16)
    return (keep[:, :rows] * inv_norm.astype(jnp.float32)).T


def solution(mesh):
    return jax.shard_map(
        per_device,
        mesh=mesh,
        in_specs=(P("dp", "feat"), P("dp"), P("dp"), P("dp")),
        out_specs=P("dp", "feat"),
        check_vma=False,
    )
```

```python
import functools

import jax
import jax.numpy as jnp
from jax import lax
from jax.experimental import pallas as pl
from jax.experimental.pallas import tpu as pltpu
from jax.sharding import PartitionSpec as P

CAND_DEV = 1
PER_PROMPT = 16
LANES = 128
VMEM_LIMIT = 32 * 1024 * 1024

epsilon = 1e-06

VMEM = pl.BlockSpec(memory_space=pltpu.VMEM)
HBM = pl.BlockSpec(memory_space=pltpu.HBM)


def in_hbm(value):
    return pltpu.with_memory_space_constraint(value, pltpu.HBM)


def sums_kernel(
    steps, counts_ref, cand_hbm, labels_hbm, acts_hbm, sums_ref, acts_ref,
    cand_ref, labels_ref, small_sems, sems,
):
    rows, width = acts_ref.shape
    classes = sums_ref.shape[0]
    cands = classes // 2
    prompts = labels_ref.shape[1]
    tall = rows // steps

    small = [
        pltpu.make_async_copy(source, target, small_sems.at[place])
        for place, (source, target) in enumerate(
            ((cand_hbm, cand_ref), (labels_hbm, labels_ref))
        )
    ]

    def fetch(step):
        part = pl.ds(step * tall, tall)
        return pltpu.make_async_copy(acts_hbm.at[part, :], acts_ref.at[part, :], sems.at[step])

    for copy in small:
        copy.start()
    for step in range(steps):
        fetch(step).start()

    prompt_ids = lax.broadcasted_iota(jnp.int32, (prompts, rows), 0)
    prompt_of = lax.broadcasted_iota(jnp.int32, (prompts, rows), 1) // PER_PROMPT
    spread = jnp.where(prompt_ids == prompt_of, 1.0, 0.0).astype(jnp.bfloat16)
    wanted = lax.broadcasted_iota(jnp.int32, (classes, rows), 0)
    row_prompt = lax.broadcasted_iota(jnp.int32, (1, rows), 1) // PER_PROMPT
    for copy in small:
        copy.wait()
    labels = jnp.broadcast_to(labels_ref[...].astype(jnp.float32), (8, prompts))
    row_class = jnp.dot(labels.astype(jnp.bfloat16), spread, preferred_element_type=jnp.float32)[:1]
    slot = jnp.where(row_class == 1.0, cand_ref[...], cand_ref[...] + cands)
    slot = jnp.where(row_prompt < counts_ref[0], slot, -1)
    member_float = jnp.where(wanted == slot, 1.0, 0.0)
    member = member_float.astype(jnp.bfloat16)
    tally = jnp.sum(member_float, axis=1, keepdims=True)
    sums_ref[:, width:] = jnp.broadcast_to(tally, (classes, LANES))

    total = None
    for step in range(steps):
        fetch(step).wait()
        piece = jnp.dot(
            member[:, step * tall : (step + 1) * tall],
            acts_ref[step * tall : (step + 1) * tall, :],
            preferred_element_type=jnp.float32,
        )
        total = piece if total is None else total + piece
    sums_ref[:, :width] = total


def class_sums(activations, cand_index, labels, counts, classes, steps=8):
    rows, width = activations.shape
    prompts = labels.shape[0]
    return pl.pallas_call(
        functools.partial(sums_kernel, steps),
        out_shape=(
            jax.ShapeDtypeStruct((classes, width + LANES), jnp.float32),
            pltpu.VMEM((rows, width), activations.dtype),
        ),
        in_specs=[pl.BlockSpec(memory_space=pltpu.SMEM)] + [HBM] * 3,
        out_specs=(VMEM, VMEM),
        scratch_shapes=[
            pltpu.VMEM((1, rows), jnp.int32),
            pltpu.VMEM((1, prompts), jnp.int32),
            pltpu.SemaphoreType.DMA((2,)),
            pltpu.SemaphoreType.DMA((steps,)),
        ],
        compiler_params=pltpu.CompilerParams(vmem_limit_bytes=VMEM_LIMIT),
        name="class_sums",
    )(
        counts,
        in_hbm(cand_index.reshape(1, rows)),
        in_hbm(labels.reshape(1, prompts)),
        in_hbm(activations),
    )


def project_kernel(mine_ref, other_ref, acts_ref, keep_ref, *send_refs):
    rows, width = acts_ref.shape
    cands = mine_ref.shape[0] // 2
    parts = len(send_refs) + 1
    part = cands // parts
    place = lax.axis_index("feat")
    total = mine_ref[...] + other_ref[...]
    tally = jnp.maximum(total[:, width : width + 1], 1.0)
    harmful_mean = total[:cands, :width] / tally[:cands]
    harmless_mean = total[cands:, :width] / tally[cands:]
    raw_dir = (harmful_mean - harmless_mean).astype(jnp.bfloat16)
    squares = jnp.sum(jnp.square(raw_dir.astype(jnp.float32)), axis=1, keepdims=True)
    squares = jnp.broadcast_to(squares, (cands, LANES))
    plain = lax.dot_general(
        raw_dir, acts_ref[...], (((1,), (1,)), ((), ())), preferred_element_type=jnp.float32
    )
    for step, out_ref in enumerate((keep_ref,) + send_refs):
        for value, columns in ((plain, slice(0, rows)), (squares, slice(rows, rows + LANES))):
            chosen = value[:part]
            for block in range(1, parts):
                mine = place == block ^ step
                chosen = jnp.where(mine, value[block * part : (block + 1) * part], chosen)
            out_ref[:, columns] = chosen


def project(mine, other, acts):
    rows = acts.shape[0]
    parts = lax.axis_size("feat")
    part = jax.ShapeDtypeStruct((mine.shape[0] // 2 // parts, rows + LANES), jnp.float32)
    return pl.pallas_call(
        project_kernel,
        out_shape=(part,) * parts,
        in_specs=[VMEM] * 3,
        out_specs=(VMEM,) * parts,
        compiler_params=pltpu.CompilerParams(vmem_limit_bytes=VMEM_LIMIT),
        name="project",
    )(mine, other, pltpu.with_memory_space_constraint(acts, pltpu.VMEM))


def scale_kernel(*refs):
    *share_refs, scores_ref = refs
    rows = scores_ref.shape[1]
    total = share_refs[0][...]
    for ref in share_refs[1:]:
        total = total + ref[...]
    inv_norm = lax.rsqrt(total[:, rows : rows + 1] + epsilon).astype(jnp.bfloat16)
    scores_ref[...] = total[:, :rows] * inv_norm.astype(jnp.float32)


def scale(shares):
    part, columns = shares[0].shape
    return pl.pallas_call(
        scale_kernel,
        out_shape=jax.ShapeDtypeStruct((part, columns - LANES), jnp.float32),
        in_specs=[VMEM] * len(shares),
        out_specs=VMEM,
        compiler_params=pltpu.CompilerParams(vmem_limit_bytes=VMEM_LIMIT),
        name="scale",
    )(*shares)


def dp_trade(value, step):
    dp, feat = lax.axis_size("dp"), lax.axis_size("feat")
    bits = [1 << b for b in range(dp.bit_length() - 1)]
    bits = bits[:1] + bits[:0:-1]
    pairs = []
    for d in range(dp):
        for f in range(feat):
            bit = bits[(step + f % 2) % len(bits)]
            pairs.append((d * feat + f, (d ^ bit) * feat + f))
    return lax.ppermute(value, ("dp", "feat"), pairs)


def feat_trade(value, bits):
    return lax.ppermute(value, "feat", [(f, f ^ bits) for f in range(lax.axis_size("feat"))])


def per_device(activations, cand_index, labels, counts):
    dp, feat = lax.axis_size("dp"), lax.axis_size("feat")
    sums, acts = class_sums(activations, cand_index, labels, counts, 2 * CAND_DEV * dp)
    rounds = dp.bit_length() - 1
    for step in range(rounds - 1):
        sums = sums + dp_trade(sums, step)
    keep, *sends = project(sums, dp_trade(sums, rounds - 1), acts)
    shares = [feat_trade(sends[bits - 1], bits) for bits in range(feat - 1, 0, -1)]
    return scale([keep] + shares).T


def solution(mesh):
    return jax.shard_map(
        per_device,
        mesh=mesh,
        in_specs=(P("dp", "feat"), P("dp"), P("dp"), P("dp")),
        out_specs=P("dp", "feat"),
        check_vma=False,
    )
```

```python
import functools

import jax
import jax.numpy as jnp
from jax import lax
from jax.experimental import pallas as pl
from jax.experimental.pallas import tpu as pltpu
from jax.sharding import PartitionSpec as P

CAND_DEV = 1
PER_PROMPT = 16
LANES = 128
VMEM_LIMIT = 32 * 1024 * 1024

epsilon = 1e-06

VMEM = pl.BlockSpec(memory_space=pltpu.VMEM)
HBM = pl.BlockSpec(memory_space=pltpu.HBM)


def in_hbm(value):
    return pltpu.with_memory_space_constraint(value, pltpu.HBM)


def in_vmem(value):
    return pltpu.with_memory_space_constraint(value, pltpu.VMEM)


def sums_kernel(
    steps, counts_ref, cand_hbm, labels_hbm, acts_hbm, sums_ref, member_ref, acts_ref,
    cand_ref, labels_ref, small_sems, sems,
):
    rows = acts_ref.shape[0]
    classes = sums_ref.shape[0]
    first = sums_ref.shape[1] - LANES
    cands = classes // 2
    prompts = labels_ref.shape[1]
    tall = rows // steps

    small = [
        pltpu.make_async_copy(source, target, small_sems.at[place])
        for place, (source, target) in enumerate(
            ((cand_hbm, cand_ref), (labels_hbm, labels_ref))
        )
    ]

    def fetch(step):
        part = pl.ds(step * tall, tall)
        return pltpu.make_async_copy(acts_hbm.at[part, :], acts_ref.at[part, :], sems.at[step])

    for copy in small:
        copy.start()
    for step in range(steps):
        fetch(step).start()

    prompt_ids = lax.broadcasted_iota(jnp.int32, (prompts, rows), 0)
    prompt_of = lax.broadcasted_iota(jnp.int32, (prompts, rows), 1) // PER_PROMPT
    spread = jnp.where(prompt_ids == prompt_of, 1.0, 0.0).astype(jnp.bfloat16)
    wanted = lax.broadcasted_iota(jnp.int32, (classes, rows), 0)
    row_prompt = lax.broadcasted_iota(jnp.int32, (1, rows), 1) // PER_PROMPT
    for copy in small:
        copy.wait()
    labels = jnp.broadcast_to(labels_ref[...].astype(jnp.float32), (8, prompts))
    row_class = jnp.dot(labels.astype(jnp.bfloat16), spread, preferred_element_type=jnp.float32)[:1]
    slot = jnp.where(row_class == 1.0, cand_ref[...], cand_ref[...] + cands)
    slot = jnp.where(row_prompt < counts_ref[0], slot, -1)
    member_float = jnp.where(wanted == slot, 1.0, 0.0)
    member = member_float.astype(jnp.bfloat16)
    member_ref[...] = member
    tally = jnp.sum(member_float, axis=1, keepdims=True)
    sums_ref[:, first:] = jnp.broadcast_to(tally, (classes, LANES))

    total = None
    for step in range(steps):
        fetch(step).wait()
        piece = jnp.dot(
            member[:, step * tall : (step + 1) * tall],
            acts_ref[step * tall : (step + 1) * tall, :first],
            preferred_element_type=jnp.float32,
        )
        total = piece if total is None else total + piece
    sums_ref[:, :first] = total


def class_sums(activations, cand_index, labels, counts, classes, first, steps=8):
    rows, width = activations.shape
    prompts = labels.shape[0]
    return pl.pallas_call(
        functools.partial(sums_kernel, steps),
        out_shape=(
            jax.ShapeDtypeStruct((classes, first + LANES), jnp.float32),
            pltpu.VMEM((classes, rows), jnp.bfloat16),
            pltpu.VMEM((rows, width), activations.dtype),
        ),
        in_specs=[pl.BlockSpec(memory_space=pltpu.SMEM)] + [HBM] * 3,
        out_specs=(VMEM,) * 3,
        scratch_shapes=[
            pltpu.VMEM((1, rows), jnp.int32),
            pltpu.VMEM((1, prompts), jnp.int32),
            pltpu.SemaphoreType.DMA((2,)),
            pltpu.SemaphoreType.DMA((steps,)),
        ],
        compiler_params=pltpu.CompilerParams(vmem_limit_bytes=VMEM_LIMIT),
        name="class_sums",
    )(
        counts,
        in_hbm(cand_index.reshape(1, rows)),
        in_hbm(labels.reshape(1, prompts)),
        in_hbm(activations),
    )


def rest_kernel(member_ref, acts_ref, sums_ref):
    first = acts_ref.shape[1] - sums_ref.shape[1]
    sums_ref[...] = jnp.dot(
        member_ref[...], acts_ref[:, first:], preferred_element_type=jnp.float32
    )


def rest_sums(member, acts, first):
    rows, width = acts.shape
    classes = member.shape[0]
    return pl.pallas_call(
        rest_kernel,
        out_shape=jax.ShapeDtypeStruct((classes, width - first), jnp.float32),
        in_specs=[VMEM] * 2,
        out_specs=VMEM,
        cost_estimate=pl.CostEstimate(
            flops=2 * classes * rows * (width - first), bytes_accessed=2 * rows * width, transcendentals=0
        ),
        compiler_params=pltpu.CompilerParams(vmem_limit_bytes=VMEM_LIMIT),
        name="rest_sums",
    )(in_vmem(member), in_vmem(acts))


def directions(total, tally):
    cands = total.shape[0] // 2
    harmful_mean = total[:cands] / tally[:cands]
    harmless_mean = total[cands:] / tally[cands:]
    raw_dir = (harmful_mean - harmless_mean).astype(jnp.bfloat16)
    return raw_dir, jnp.sum(jnp.square(raw_dir.astype(jnp.float32)), axis=1, keepdims=True)


def project_kernel(mine_ref, other_ref, acts_ref, shares_ref, tally_ref):
    rows = acts_ref.shape[0]
    first = mine_ref.shape[1] - LANES
    total = mine_ref[...] + other_ref[...]
    tally = jnp.maximum(total[:, first:], 1.0)
    tally_ref[...] = tally
    raw_dir, squares = directions(total[:, :first], tally[:, :1])
    shares_ref[:, :rows] = lax.dot_general(
        raw_dir, acts_ref[:, :first], (((1,), (1,)), ((), ())), preferred_element_type=jnp.float32
    )
    shares_ref[:, rows:] = jnp.broadcast_to(squares, (squares.shape[0], LANES))


def project(mine, other, acts):
    rows = acts.shape[0]
    classes = mine.shape[0]
    return pl.pallas_call(
        project_kernel,
        out_shape=(
            jax.ShapeDtypeStruct((classes // 2, rows + LANES), jnp.float32),
            jax.ShapeDtypeStruct((classes, LANES), jnp.float32),
        ),
        in_specs=[VMEM] * 3,
        out_specs=(VMEM,) * 2,
        compiler_params=pltpu.CompilerParams(vmem_limit_bytes=VMEM_LIMIT),
        name="project",
    )(mine, other, in_vmem(acts))


def project_rest_kernel(mine_ref, other_ref, tally_ref, shares_ref, acts_ref, keep_ref, *send_refs):
    rows, width = acts_ref.shape
    first = width - mine_ref.shape[1]
    cands = mine_ref.shape[0] // 2
    parts = len(send_refs) + 1
    part = cands // parts
    place = lax.axis_index("feat")
    raw_dir, squares = directions(mine_ref[...] + other_ref[...], tally_ref[:, :1])
    plain = lax.dot_general(
        raw_dir, acts_ref[:, first:], (((1,), (1,)), ((), ())), preferred_element_type=jnp.float32
    )
    plain = plain + shares_ref[:, :rows]
    squares = squares + shares_ref[:, rows:]
    for step, out_ref in enumerate((keep_ref,) + send_refs):
        for value, columns in ((plain, slice(0, rows)), (squares, slice(rows, rows + LANES))):
            chosen = value[:part]
            for block in range(1, parts):
                mine = place == block ^ step
                chosen = jnp.where(mine, value[block * part : (block + 1) * part], chosen)
            out_ref[:, columns] = chosen


def project_rest(mine, other, tally, shares, acts):
    rows = acts.shape[0]
    parts = lax.axis_size("feat")
    part = jax.ShapeDtypeStruct((mine.shape[0] // 2 // parts, rows + LANES), jnp.float32)
    return pl.pallas_call(
        project_rest_kernel,
        out_shape=(part,) * parts,
        in_specs=[VMEM] * 5,
        out_specs=(VMEM,) * parts,
        compiler_params=pltpu.CompilerParams(vmem_limit_bytes=VMEM_LIMIT),
        name="project_rest",
    )(mine, other, tally, shares, in_vmem(acts))


def scale_kernel(*refs):
    *share_refs, scores_ref = refs
    rows = scores_ref.shape[1]
    total = share_refs[0][...]
    for ref in share_refs[1:]:
        total = total + ref[...]
    inv_norm = lax.rsqrt(total[:, rows : rows + 1] + epsilon).astype(jnp.bfloat16)
    scores_ref[...] = total[:, :rows] * inv_norm.astype(jnp.float32)


def scale(shares):
    part, columns = shares[0].shape
    return pl.pallas_call(
        scale_kernel,
        out_shape=jax.ShapeDtypeStruct((part, columns - LANES), jnp.float32),
        in_specs=[VMEM] * len(shares),
        out_specs=VMEM,
        compiler_params=pltpu.CompilerParams(vmem_limit_bytes=VMEM_LIMIT),
        name="scale",
    )(*shares)


def dp_trade(value, step):
    dp, feat = lax.axis_size("dp"), lax.axis_size("feat")
    bits = [1 << b for b in range(dp.bit_length() - 1)]
    bits = bits[:1] + bits[:0:-1]
    pairs = []
    for d in range(dp):
        for f in range(feat):
            bit = bits[(step + f % 2) % len(bits)]
            pairs.append((d * feat + f, (d ^ bit) * feat + f))
    return lax.ppermute(value, ("dp", "feat"), pairs)


def feat_trade(value, bits):
    return lax.ppermute(value, "feat", [(f, f ^ bits) for f in range(lax.axis_size("feat"))])


def per_device(activations, cand_index, labels, counts):
    dp, feat = lax.axis_size("dp"), lax.axis_size("feat")
    first = activations.shape[1] // 2
    sums, member, acts = class_sums(
        activations, cand_index, labels, counts, 2 * CAND_DEV * dp, first
    )
    rest = rest_sums(member, acts, first)
    rounds = dp.bit_length() - 1
    for step in range(rounds - 1):
        sums = sums + dp_trade(sums, step)
        rest = rest + dp_trade(rest, step)
    shares, tally = project(sums, dp_trade(sums, rounds - 1), acts)
    keep, *sends = project_rest(rest, dp_trade(rest, rounds - 1), tally, shares, acts)
    shares = [feat_trade(sends[bits - 1], bits) for bits in range(feat - 1, 0, -1)]
    return scale([keep] + shares).T


def solution(mesh):
    return jax.shard_map(
        per_device,
        mesh=mesh,
        in_specs=(P("dp", "feat"), P("dp"), P("dp"), P("dp")),
        out_specs=P("dp", "feat"),
        check_vma=False,
    )
```

```python
import jax
import jax.numpy as jnp
from jax import lax
from jax.experimental import pallas as pl
from jax.experimental.pallas import tpu as pltpu
from jax.sharding import PartitionSpec as P

CAND_DEV = 1
PER_PROMPT = 16
LANES = 128
VMEM_LIMIT = 32 * 1024 * 1024

epsilon = 1e-06

VMEM = pl.BlockSpec(memory_space=pltpu.VMEM)
HBM = pl.BlockSpec(memory_space=pltpu.HBM)


def in_hbm(value):
    return pltpu.with_memory_space_constraint(value, pltpu.HBM)


def in_vmem(value):
    return pltpu.with_memory_space_constraint(value, pltpu.VMEM)


def sums_kernel(
    counts_ref, cand_hbm, labels_hbm, acts_hbm, sums_ref, member_ref, acts_ref,
    cand_ref, labels_ref, small_sems, sems,
):
    rows = acts_ref.shape[0]
    classes = sums_ref.shape[0]
    first = sums_ref.shape[1] - LANES
    cands = classes // 2
    prompts = labels_ref.shape[1]

    small = [
        pltpu.make_async_copy(source, target, small_sems.at[place])
        for place, (source, target) in enumerate(
            ((cand_hbm, cand_ref), (labels_hbm, labels_ref))
        )
    ]

    def fetch(part):
        columns = (pl.ds(0, first), pl.ds(first, acts_ref.shape[1] - first))[part]
        return pltpu.make_async_copy(
            acts_hbm.at[:, columns], acts_ref.at[:, columns], sems.at[part]
        )

    for copy in small:
        copy.start()
    for part in range(2):
        fetch(part).start()

    prompt_ids = lax.broadcasted_iota(jnp.int32, (prompts, rows), 0)
    prompt_of = lax.broadcasted_iota(jnp.int32, (prompts, rows), 1) // PER_PROMPT
    spread = jnp.where(prompt_ids == prompt_of, 1.0, 0.0).astype(jnp.bfloat16)
    wanted = lax.broadcasted_iota(jnp.int32, (classes, rows), 0)
    row_prompt = lax.broadcasted_iota(jnp.int32, (1, rows), 1) // PER_PROMPT
    for copy in small:
        copy.wait()
    labels = jnp.broadcast_to(labels_ref[...].astype(jnp.float32), (8, prompts))
    row_class = jnp.dot(labels.astype(jnp.bfloat16), spread, preferred_element_type=jnp.float32)[:1]
    slot = jnp.where(row_class == 1.0, cand_ref[...], cand_ref[...] + cands)
    slot = jnp.where(row_prompt < counts_ref[0], slot, -1)
    member_float = jnp.where(wanted == slot, 1.0, 0.0)
    member = member_float.astype(jnp.bfloat16)
    member_ref[...] = member
    tally = jnp.sum(member_float, axis=1, keepdims=True)
    sums_ref[:, first:] = jnp.broadcast_to(tally, (classes, LANES))

    fetch(0).wait()
    sums_ref[:, :first] = jnp.dot(
        member, acts_ref[:, :first], preferred_element_type=jnp.float32
    )
    fetch(1).wait()


def class_sums(activations, cand_index, labels, counts, classes, first):
    rows, width = activations.shape
    prompts = labels.shape[0]
    return pl.pallas_call(
        sums_kernel,
        out_shape=(
            jax.ShapeDtypeStruct((classes, first + LANES), jnp.float32),
            pltpu.VMEM((classes, rows), jnp.bfloat16),
            pltpu.VMEM((rows, width), activations.dtype),
        ),
        in_specs=[pl.BlockSpec(memory_space=pltpu.SMEM)] + [HBM] * 3,
        out_specs=(VMEM,) * 3,
        scratch_shapes=[
            pltpu.VMEM((1, rows), jnp.int32),
            pltpu.VMEM((1, prompts), jnp.int32),
            pltpu.SemaphoreType.DMA((2,)),
            pltpu.SemaphoreType.DMA((2,)),
        ],
        compiler_params=pltpu.CompilerParams(vmem_limit_bytes=VMEM_LIMIT),
        name="class_sums",
    )(
        counts,
        in_hbm(cand_index.reshape(1, rows)),
        in_hbm(labels.reshape(1, prompts)),
        in_hbm(activations),
    )


def rest_kernel(member_ref, acts_ref, sums_ref):
    first = acts_ref.shape[1] - sums_ref.shape[1]
    sums_ref[...] = jnp.dot(
        member_ref[...], acts_ref[:, first:], preferred_element_type=jnp.float32
    )


def rest_sums(member, acts, first):
    rows, width = acts.shape
    classes = member.shape[0]
    return pl.pallas_call(
        rest_kernel,
        out_shape=jax.ShapeDtypeStruct((classes, width - first), jnp.float32),
        in_specs=[VMEM] * 2,
        out_specs=VMEM,
        cost_estimate=pl.CostEstimate(
            flops=2 * classes * rows * (width - first), bytes_accessed=2 * rows * width, transcendentals=0
        ),
        compiler_params=pltpu.CompilerParams(vmem_limit_bytes=VMEM_LIMIT),
        name="rest_sums",
    )(in_vmem(member), in_vmem(acts))


def directions(total, tally):
    cands = total.shape[0] // 2
    harmful_mean = total[:cands] / tally[:cands]
    harmless_mean = total[cands:] / tally[cands:]
    raw_dir = (harmful_mean - harmless_mean).astype(jnp.bfloat16)
    return raw_dir, jnp.sum(jnp.square(raw_dir.astype(jnp.float32)), axis=1, keepdims=True)


def project_kernel(mine_ref, other_ref, acts_ref, shares_ref, tally_ref):
    rows = acts_ref.shape[0]
    first = mine_ref.shape[1] - LANES
    total = mine_ref[...] + other_ref[...]
    tally = jnp.maximum(total[:, first:], 1.0)
    tally_ref[...] = tally
    raw_dir, squares = directions(total[:, :first], tally[:, :1])
    shares_ref[:, :rows] = lax.dot_general(
        raw_dir, acts_ref[:, :first], (((1,), (1,)), ((), ())), preferred_element_type=jnp.float32
    )
    shares_ref[:, rows:] = jnp.broadcast_to(squares, (squares.shape[0], LANES))


def project(mine, other, acts):
    rows = acts.shape[0]
    classes = mine.shape[0]
    return pl.pallas_call(
        project_kernel,
        out_shape=(
            jax.ShapeDtypeStruct((classes // 2, rows + LANES), jnp.float32),
            jax.ShapeDtypeStruct((classes, LANES), jnp.float32),
        ),
        in_specs=[VMEM] * 3,
        out_specs=(VMEM,) * 2,
        compiler_params=pltpu.CompilerParams(vmem_limit_bytes=VMEM_LIMIT),
        name="project",
    )(mine, other, in_vmem(acts))


def project_rest_kernel(mine_ref, other_ref, tally_ref, shares_ref, acts_ref, keep_ref, *send_refs):
    rows, width = acts_ref.shape
    first = width - mine_ref.shape[1]
    cands = mine_ref.shape[0] // 2
    parts = len(send_refs) + 1
    part = cands // parts
    place = lax.axis_index("feat")
    raw_dir, squares = directions(mine_ref[...] + other_ref[...], tally_ref[:, :1])
    plain = lax.dot_general(
        raw_dir, acts_ref[:, first:], (((1,), (1,)), ((), ())), preferred_element_type=jnp.float32
    )
    plain = plain + shares_ref[:, :rows]
    squares = squares + shares_ref[:, rows:]
    for step, out_ref in enumerate((keep_ref,) + send_refs):
        for value, columns in ((plain, slice(0, rows)), (squares, slice(rows, rows + LANES))):
            chosen = value[:part]
            for block in range(1, parts):
                mine = place == block ^ step
                chosen = jnp.where(mine, value[block * part : (block + 1) * part], chosen)
            out_ref[:, columns] = chosen


def project_rest(mine, other, tally, shares, acts):
    rows = acts.shape[0]
    parts = lax.axis_size("feat")
    part = jax.ShapeDtypeStruct((mine.shape[0] // 2 // parts, rows + LANES), jnp.float32)
    return pl.pallas_call(
        project_rest_kernel,
        out_shape=(part,) * parts,
        in_specs=[VMEM] * 5,
        out_specs=(VMEM,) * parts,
        compiler_params=pltpu.CompilerParams(vmem_limit_bytes=VMEM_LIMIT),
        name="project_rest",
    )(mine, other, tally, shares, in_vmem(acts))


def scale_kernel(*refs):
    *share_refs, scores_ref = refs
    rows = scores_ref.shape[1]
    total = share_refs[0][...]
    for ref in share_refs[1:]:
        total = total + ref[...]
    inv_norm = lax.rsqrt(total[:, rows : rows + 1] + epsilon).astype(jnp.bfloat16)
    scores_ref[...] = total[:, :rows] * inv_norm.astype(jnp.float32)


def scale(shares):
    part, columns = shares[0].shape
    return pl.pallas_call(
        scale_kernel,
        out_shape=jax.ShapeDtypeStruct((part, columns - LANES), jnp.float32),
        in_specs=[VMEM] * len(shares),
        out_specs=VMEM,
        compiler_params=pltpu.CompilerParams(vmem_limit_bytes=VMEM_LIMIT),
        name="scale",
    )(*shares)


def dp_trade(value, step, half):
    dp, feat = lax.axis_size("dp"), lax.axis_size("feat")
    count = dp.bit_length() - 1
    up = list(range(count))
    even = (up, up[:1] + up[:0:-1])[half]
    odd = up[-1:] + up[:-1]
    pairs = []
    for d in range(dp):
        for f in range(feat):
            bit = 1 << (odd if f % 2 else even)[step]
            pairs.append((d * feat + f, (d ^ bit) * feat + f))
    return lax.ppermute(value, ("dp", "feat"), pairs)


def feat_trade(value, bits):
    return lax.ppermute(value, "feat", [(f, f ^ bits) for f in range(lax.axis_size("feat"))])


def per_device(activations, cand_index, labels, counts):
    dp, feat = lax.axis_size("dp"), lax.axis_size("feat")
    first = activations.shape[1] // 2
    sums, member, acts = class_sums(
        activations, cand_index, labels, counts, 2 * CAND_DEV * dp, first
    )
    rest = rest_sums(member, acts, first)
    rounds = dp.bit_length() - 1
    for step in range(rounds - 1):
        sums = sums + dp_trade(sums, step, 0)
        rest = rest + dp_trade(rest, step, 1)
    shares, tally = project(sums, dp_trade(sums, rounds - 1, 0), acts)
    keep, *sends = project_rest(rest, dp_trade(rest, rounds - 1, 1), tally, shares, acts)
    shares = [feat_trade(sends[bits - 1], bits) for bits in range(feat - 1, 0, -1)]
    return scale([keep] + shares).T


def solution(mesh):
    return jax.shard_map(
        per_device,
        mesh=mesh,
        in_specs=(P("dp", "feat"), P("dp"), P("dp"), P("dp")),
        out_specs=P("dp", "feat"),
        check_vma=False,
    )
```

```python
import jax
import jax.numpy as jnp
from jax import lax
from jax.experimental import pallas as pl
from jax.experimental.pallas import tpu as pltpu
from jax.sharding import PartitionSpec as P

CAND_DEV = 1
PER_PROMPT = 16
LANES = 128
VMEM_LIMIT = 32 * 1024 * 1024

epsilon = 1e-06

VMEM = pl.BlockSpec(memory_space=pltpu.VMEM)
HBM = pl.BlockSpec(memory_space=pltpu.HBM)


def in_hbm(value):
    return pltpu.with_memory_space_constraint(value, pltpu.HBM)


def in_vmem(value):
    return pltpu.with_memory_space_constraint(value, pltpu.VMEM)


def member_kernel(counts_ref, cand_hbm, labels_hbm, member_ref, tally_ref, cand_ref, labels_ref, sems):
    classes, rows = member_ref.shape
    cands = classes // 2
    prompts = labels_ref.shape[1]
    copies = [
        pltpu.make_async_copy(source, target, sems.at[place])
        for place, (source, target) in enumerate(
            ((cand_hbm, cand_ref), (labels_hbm, labels_ref))
        )
    ]
    for copy in copies:
        copy.start()
    prompt_ids = lax.broadcasted_iota(jnp.int32, (prompts, rows), 0)
    prompt_of = lax.broadcasted_iota(jnp.int32, (prompts, rows), 1) // PER_PROMPT
    spread = jnp.where(prompt_ids == prompt_of, 1.0, 0.0).astype(jnp.bfloat16)
    wanted = lax.broadcasted_iota(jnp.int32, (classes, rows), 0)
    row_prompt = lax.broadcasted_iota(jnp.int32, (1, rows), 1) // PER_PROMPT
    for copy in copies:
        copy.wait()
    labels = jnp.broadcast_to(labels_ref[...].astype(jnp.float32), (8, prompts))
    row_class = jnp.dot(labels.astype(jnp.bfloat16), spread, preferred_element_type=jnp.float32)[:1]
    slot = jnp.where(row_class == 1.0, cand_ref[...], cand_ref[...] + cands)
    slot = jnp.where(row_prompt < counts_ref[0], slot, -1)
    member = jnp.where(wanted == slot, 1.0, 0.0)
    member_ref[...] = member.astype(jnp.bfloat16)
    tally = jnp.sum(member, axis=1, keepdims=True)
    tally_ref[...] = jnp.broadcast_to(tally, (classes, LANES))


def membership(cand_index, labels, counts, classes, width):
    rows, prompts = cand_index.shape[0], labels.shape[0]
    return pl.pallas_call(
        member_kernel,
        out_shape=(
            jax.ShapeDtypeStruct((classes, rows), jnp.bfloat16),
            jax.ShapeDtypeStruct((classes, LANES), jnp.float32),
        ),
        in_specs=[pl.BlockSpec(memory_space=pltpu.SMEM)] + [HBM] * 2,
        out_specs=(VMEM,) * 2,
        scratch_shapes=[
            pltpu.VMEM((1, rows), jnp.int32),
            pltpu.VMEM((1, prompts), jnp.int32),
            pltpu.SemaphoreType.DMA((2,)),
        ],
        cost_estimate=pl.CostEstimate(flops=800 * rows * width, bytes_accessed=0, transcendentals=0),
        compiler_params=pltpu.CompilerParams(vmem_limit_bytes=VMEM_LIMIT),
        name="membership",
    )(counts, in_hbm(cand_index.reshape(1, rows)), in_hbm(labels.reshape(1, prompts)))


def first_kernel(member_ref, tally_ref, acts_ref, sums_ref):
    first = sums_ref.shape[1] - LANES
    sums_ref[:, :first] = jnp.dot(
        member_ref[...], acts_ref[:, :first], preferred_element_type=jnp.float32
    )
    sums_ref[:, first:] = tally_ref[...]


def first_sums(member, tally, acts, first):
    return pl.pallas_call(
        first_kernel,
        out_shape=jax.ShapeDtypeStruct((member.shape[0], first + LANES), jnp.float32),
        in_specs=[VMEM] * 3,
        out_specs=VMEM,
        compiler_params=pltpu.CompilerParams(vmem_limit_bytes=VMEM_LIMIT),
        name="first_sums",
    )(in_vmem(member), in_vmem(tally), acts)


def rest_kernel(member_ref, acts_ref, sums_ref):
    first = acts_ref.shape[1] - sums_ref.shape[1]
    sums_ref[...] = jnp.dot(
        member_ref[...], acts_ref[:, first:], preferred_element_type=jnp.float32
    )


def rest_sums(member, acts, first):
    return pl.pallas_call(
        rest_kernel,
        out_shape=jax.ShapeDtypeStruct((member.shape[0], acts.shape[1] - first), jnp.float32),
        in_specs=[VMEM] * 2,
        out_specs=VMEM,
        compiler_params=pltpu.CompilerParams(vmem_limit_bytes=VMEM_LIMIT),
        name="rest_sums",
    )(in_vmem(member), acts)


def directions(total, tally):
    cands = total.shape[0] // 2
    harmful_mean = total[:cands] / tally[:cands]
    harmless_mean = total[cands:] / tally[cands:]
    raw_dir = (harmful_mean - harmless_mean).astype(jnp.bfloat16)
    return raw_dir, jnp.sum(jnp.square(raw_dir.astype(jnp.float32)), axis=1, keepdims=True)


def project_kernel(mine_ref, other_ref, acts_ref, shares_ref, tally_ref):
    rows = acts_ref.shape[0]
    first = mine_ref.shape[1] - LANES
    total = mine_ref[...] + other_ref[...]
    tally = jnp.maximum(total[:, first:], 1.0)
    tally_ref[...] = tally
    raw_dir, squares = directions(total[:, :first], tally[:, :1])
    shares_ref[:, :rows] = lax.dot_general(
        raw_dir, acts_ref[:, :first], (((1,), (1,)), ((), ())), preferred_element_type=jnp.float32
    )
    shares_ref[:, rows:] = jnp.broadcast_to(squares, (squares.shape[0], LANES))


def project(mine, other, acts):
    rows = acts.shape[0]
    classes = mine.shape[0]
    return pl.pallas_call(
        project_kernel,
        out_shape=(
            jax.ShapeDtypeStruct((classes // 2, rows + LANES), jnp.float32),
            jax.ShapeDtypeStruct((classes, LANES), jnp.float32),
        ),
        in_specs=[VMEM] * 3,
        out_specs=(VMEM,) * 2,
        compiler_params=pltpu.CompilerParams(vmem_limit_bytes=VMEM_LIMIT),
        name="project",
    )(mine, other, acts)


def project_rest_kernel(mine_ref, other_ref, tally_ref, shares_ref, acts_ref, keep_ref, *send_refs):
    rows = acts_ref.shape[0]
    cands = mine_ref.shape[0] // 2
    parts = len(send_refs) + 1
    part = cands // parts
    place = lax.axis_index("feat")
    raw_dir, squares = directions(mine_ref[...] + other_ref[...], tally_ref[:, :1])
    plain = lax.dot_general(
        raw_dir, acts_ref[:, acts_ref.shape[1] - mine_ref.shape[1]:], (((1,), (1,)), ((), ())), preferred_element_type=jnp.float32
    )
    plain = plain + shares_ref[:, :rows]
    squares = squares + shares_ref[:, rows:]
    for step, out_ref in enumerate((keep_ref,) + send_refs):
        for value, columns in ((plain, slice(0, rows)), (squares, slice(rows, rows + LANES))):
            chosen = value[:part]
            for block in range(1, parts):
                mine = place == block ^ step
                chosen = jnp.where(mine, value[block * part : (block + 1) * part], chosen)
            out_ref[:, columns] = chosen


def project_rest(mine, other, tally, shares, acts):
    rows = acts.shape[0]
    parts = lax.axis_size("feat")
    part = jax.ShapeDtypeStruct((mine.shape[0] // 2 // parts, rows + LANES), jnp.float32)
    return pl.pallas_call(
        project_rest_kernel,
        out_shape=(part,) * parts,
        in_specs=[VMEM] * 5,
        out_specs=(VMEM,) * parts,
        compiler_params=pltpu.CompilerParams(vmem_limit_bytes=VMEM_LIMIT),
        name="project_rest",
    )(mine, other, tally, shares, acts)


def scale_kernel(*refs):
    *share_refs, scores_ref = refs
    rows = scores_ref.shape[1]
    total = share_refs[0][...]
    for ref in share_refs[1:]:
        total = total + ref[...]
    inv_norm = lax.rsqrt(total[:, rows : rows + 1] + epsilon).astype(jnp.bfloat16)
    scores_ref[...] = total[:, :rows] * inv_norm.astype(jnp.float32)


def scale(shares):
    part, columns = shares[0].shape
    return pl.pallas_call(
        scale_kernel,
        out_shape=jax.ShapeDtypeStruct((part, columns - LANES), jnp.float32),
        in_specs=[VMEM] * len(shares),
        out_specs=VMEM,
        compiler_params=pltpu.CompilerParams(vmem_limit_bytes=VMEM_LIMIT),
        name="scale",
    )(*shares)


def dp_trade(value, step, half):
    dp, feat = lax.axis_size("dp"), lax.axis_size("feat")
    count = dp.bit_length() - 1
    up = list(range(count))
    even = (up, up[:1] + up[:0:-1])[half]
    odd = up[-1:] + up[:-1]
    pairs = []
    for d in range(dp):
        for f in range(feat):
            bit = 1 << (odd if f % 2 else even)[step]
            pairs.append((d * feat + f, (d ^ bit) * feat + f))
    return lax.ppermute(value, ("dp", "feat"), pairs)


def feat_trade(value, bits):
    return lax.ppermute(value, "feat", [(f, f ^ bits) for f in range(lax.axis_size("feat"))])


def per_device(activations, cand_index, labels, counts):
    dp, feat = lax.axis_size("dp"), lax.axis_size("feat")
    first = activations.shape[1] // 2
    classes = 2 * CAND_DEV * dp
    acts = in_vmem(activations)
    member, tally = membership(cand_index, labels, counts, classes, activations.shape[1])
    sums = first_sums(member, tally, acts, first)
    rest = rest_sums(member, acts, first)
    rounds = dp.bit_length() - 1
    for step in range(rounds - 1):
        sums = sums + dp_trade(sums, step, 0)
        rest = rest + dp_trade(rest, step, 1)
    shares, tally = project(sums, dp_trade(sums, rounds - 1, 0), acts)
    keep, *sends = project_rest(rest, dp_trade(rest, rounds - 1, 1), tally, shares, acts)
    shares = [feat_trade(sends[bits - 1], bits) for bits in range(feat - 1, 0, -1)]
    return scale([keep] + shares).T


def solution(mesh):
    return jax.shard_map(
        per_device,
        mesh=mesh,
        in_specs=(P("dp", "feat"), P("dp"), P("dp"), P("dp")),
        out_specs=P("dp", "feat"),
        check_vma=False,
    )
```

```python
import jax
import jax.numpy as jnp
from jax import lax
from jax.experimental import pallas as pl
from jax.experimental.pallas import tpu as pltpu
from jax.sharding import PartitionSpec as P

CAND_DEV = 1
PER_PROMPT = 16
LANES = 128
VMEM_LIMIT = 32 * 1024 * 1024

epsilon = 1e-06

VMEM = pl.BlockSpec(memory_space=pltpu.VMEM)
HBM = pl.BlockSpec(memory_space=pltpu.HBM)


def in_hbm(value):
    return pltpu.with_memory_space_constraint(value, pltpu.HBM)


def in_vmem(value):
    return pltpu.with_memory_space_constraint(value, pltpu.VMEM)


def member_kernel(counts_ref, cand_hbm, labels_hbm, member_ref, tally_ref, cand_ref, labels_ref, sems):
    classes, rows = member_ref.shape
    cands = classes // 2
    prompts = labels_ref.shape[1]
    copies = [
        pltpu.make_async_copy(source, target, sems.at[place])
        for place, (source, target) in enumerate(
            ((cand_hbm, cand_ref), (labels_hbm, labels_ref))
        )
    ]
    for copy in copies:
        copy.start()
    prompt_ids = lax.broadcasted_iota(jnp.int32, (prompts, rows), 0)
    prompt_of = lax.broadcasted_iota(jnp.int32, (prompts, rows), 1) // PER_PROMPT
    spread = jnp.where(prompt_ids == prompt_of, 1.0, 0.0).astype(jnp.bfloat16)
    wanted = lax.broadcasted_iota(jnp.int32, (classes, rows), 0)
    row_prompt = lax.broadcasted_iota(jnp.int32, (1, rows), 1) // PER_PROMPT
    for copy in copies:
        copy.wait()
    labels = jnp.broadcast_to(labels_ref[...].astype(jnp.float32), (8, prompts))
    row_class = jnp.dot(labels.astype(jnp.bfloat16), spread, preferred_element_type=jnp.float32)[:1]
    slot = jnp.where(row_class == 1.0, cand_ref[...], cand_ref[...] + cands)
    slot = jnp.where(row_prompt < counts_ref[0], slot, -1)
    member = jnp.where(wanted == slot, 1.0, 0.0)
    member_ref[...] = member.astype(jnp.bfloat16)
    tally = jnp.sum(member, axis=1, keepdims=True)
    tally_ref[...] = jnp.broadcast_to(tally, (classes, LANES))


def membership(cand_index, labels, counts, classes, width):
    rows, prompts = cand_index.shape[0], labels.shape[0]
    return pl.pallas_call(
        member_kernel,
        out_shape=(
            jax.ShapeDtypeStruct((classes, rows), jnp.bfloat16),
            jax.ShapeDtypeStruct((classes, LANES), jnp.float32),
        ),
        in_specs=[pl.BlockSpec(memory_space=pltpu.SMEM)] + [HBM] * 2,
        out_specs=(VMEM,) * 2,
        scratch_shapes=[
            pltpu.VMEM((1, rows), jnp.int32),
            pltpu.VMEM((1, prompts), jnp.int32),
            pltpu.SemaphoreType.DMA((2,)),
        ],
        cost_estimate=pl.CostEstimate(flops=800 * rows * width, bytes_accessed=0, transcendentals=0),
        compiler_params=pltpu.CompilerParams(vmem_limit_bytes=VMEM_LIMIT),
        name="membership",
    )(counts, in_hbm(cand_index.reshape(1, rows)), in_hbm(labels.reshape(1, prompts)))


def first_kernel(member_ref, tally_ref, acts_ref, sums_ref):
    first = sums_ref.shape[1] - LANES
    sums_ref[:, :first] = jnp.dot(
        member_ref[...], acts_ref[:, :first], preferred_element_type=jnp.float32
    )
    sums_ref[:, first:] = tally_ref[...]


def first_sums(member, tally, acts, first):
    return pl.pallas_call(
        first_kernel,
        out_shape=jax.ShapeDtypeStruct((member.shape[0], first + LANES), jnp.float32),
        in_specs=[VMEM] * 3,
        out_specs=VMEM,
        compiler_params=pltpu.CompilerParams(vmem_limit_bytes=VMEM_LIMIT),
        name="first_sums",
    )(in_vmem(member), in_vmem(tally), acts)


def rest_kernel(member_ref, acts_ref, sums_ref):
    first = acts_ref.shape[1] - sums_ref.shape[1]
    sums_ref[...] = jnp.dot(
        member_ref[...], acts_ref[:, first:], preferred_element_type=jnp.float32
    )


def rest_sums(member, acts, first):
    return pl.pallas_call(
        rest_kernel,
        out_shape=jax.ShapeDtypeStruct((member.shape[0], acts.shape[1] - first), jnp.float32),
        in_specs=[VMEM] * 2,
        out_specs=VMEM,
        compiler_params=pltpu.CompilerParams(vmem_limit_bytes=VMEM_LIMIT),
        name="rest_sums",
    )(in_vmem(member), acts)


def directions(total, tally):
    cands = total.shape[0] // 2
    harmful_mean = total[:cands] / tally[:cands]
    harmless_mean = total[cands:] / tally[cands:]
    raw_dir = (harmful_mean - harmless_mean).astype(jnp.bfloat16)
    return raw_dir, jnp.sum(jnp.square(raw_dir.astype(jnp.float32)), axis=1, keepdims=True)


def project_kernel(mine_ref, other_ref, acts_ref, shares_ref, tally_ref):
    rows = acts_ref.shape[0]
    first = mine_ref.shape[1] - LANES
    total = mine_ref[...] + other_ref[...]
    tally = jnp.maximum(total[:, first:], 1.0)
    tally_ref[...] = tally
    raw_dir, squares = directions(total[:, :first], tally[:, :1])
    shares_ref[:, :rows] = lax.dot_general(
        raw_dir, acts_ref[:, :first], (((1,), (1,)), ((), ())), preferred_element_type=jnp.float32
    )
    shares_ref[:, rows:] = jnp.broadcast_to(squares, (squares.shape[0], LANES))


def project(mine, other, acts):
    rows = acts.shape[0]
    classes = mine.shape[0]
    return pl.pallas_call(
        project_kernel,
        out_shape=(
            jax.ShapeDtypeStruct((classes // 2, rows + LANES), jnp.float32),
            jax.ShapeDtypeStruct((classes, LANES), jnp.float32),
        ),
        in_specs=[VMEM] * 3,
        out_specs=(VMEM,) * 2,
        compiler_params=pltpu.CompilerParams(vmem_limit_bytes=VMEM_LIMIT),
        name="project",
    )(mine, other, acts)


def turn_kernel(acts_ref, turned_ref):
    first = acts_ref.shape[1] - turned_ref.shape[0]
    turned_ref[...] = acts_ref[:, first:].T


def turn(acts, first):
    rows, width = acts.shape
    return pl.pallas_call(
        turn_kernel,
        out_shape=pltpu.VMEM((width - first, rows), acts.dtype),
        in_specs=[VMEM],
        out_specs=VMEM,
        compiler_params=pltpu.CompilerParams(vmem_limit_bytes=VMEM_LIMIT),
        name="turn",
    )(acts)


def project_rest_kernel(mine_ref, other_ref, tally_ref, shares_ref, turned_ref, keep_ref, *send_refs):
    rows = turned_ref.shape[1]
    cands = mine_ref.shape[0] // 2
    parts = len(send_refs) + 1
    part = cands // parts
    place = lax.axis_index("feat")
    raw_dir, squares = directions(mine_ref[...] + other_ref[...], tally_ref[:, :1])
    plain = jnp.dot(raw_dir, turned_ref[...], preferred_element_type=jnp.float32)
    plain = plain + shares_ref[:, :rows]
    squares = squares + shares_ref[:, rows:]
    for step, out_ref in enumerate((keep_ref,) + send_refs):
        for value, columns in ((plain, slice(0, rows)), (squares, slice(rows, rows + LANES))):
            chosen = value[:part]
            for block in range(1, parts):
                mine = place == block ^ step
                chosen = jnp.where(mine, value[block * part : (block + 1) * part], chosen)
            out_ref[:, columns] = chosen


def project_rest(mine, other, tally, shares, turned):
    rows = turned.shape[1]
    parts = lax.axis_size("feat")
    part = jax.ShapeDtypeStruct((mine.shape[0] // 2 // parts, rows + LANES), jnp.float32)
    return pl.pallas_call(
        project_rest_kernel,
        out_shape=(part,) * parts,
        in_specs=[VMEM] * 5,
        out_specs=(VMEM,) * parts,
        compiler_params=pltpu.CompilerParams(vmem_limit_bytes=VMEM_LIMIT),
        name="project_rest",
    )(mine, other, tally, shares, in_vmem(turned))


def scale_kernel(*refs):
    *share_refs, scores_ref = refs
    rows = scores_ref.shape[1]
    total = share_refs[0][...]
    for ref in share_refs[1:]:
        total = total + ref[...]
    inv_norm = lax.rsqrt(total[:, rows : rows + 1] + epsilon).astype(jnp.bfloat16)
    scores_ref[...] = total[:, :rows] * inv_norm.astype(jnp.float32)


def scale(shares):
    part, columns = shares[0].shape
    return pl.pallas_call(
        scale_kernel,
        out_shape=jax.ShapeDtypeStruct((part, columns - LANES), jnp.float32),
        in_specs=[VMEM] * len(shares),
        out_specs=VMEM,
        compiler_params=pltpu.CompilerParams(vmem_limit_bytes=VMEM_LIMIT),
        name="scale",
    )(*shares)


def dp_trade(value, step, half):
    dp, feat = lax.axis_size("dp"), lax.axis_size("feat")
    count = dp.bit_length() - 1
    up = list(range(count))
    even = (up, up[:1] + up[:0:-1])[half]
    odd = up[-1:] + up[:-1]
    pairs = []
    for d in range(dp):
        for f in range(feat):
            bit = 1 << (odd if f % 2 else even)[step]
            pairs.append((d * feat + f, (d ^ bit) * feat + f))
    return lax.ppermute(value, ("dp", "feat"), pairs)


def feat_trade(value, bits):
    return lax.ppermute(value, "feat", [(f, f ^ bits) for f in range(lax.axis_size("feat"))])


def per_device(activations, cand_index, labels, counts):
    dp, feat = lax.axis_size("dp"), lax.axis_size("feat")
    first = activations.shape[1] // 2
    classes = 2 * CAND_DEV * dp
    acts = in_vmem(activations)
    member, tally = membership(cand_index, labels, counts, classes, activations.shape[1])
    sums = first_sums(member, tally, acts, first)
    rest = rest_sums(member, acts, first)
    rounds = dp.bit_length() - 1
    for step in range(rounds - 1):
        sums = sums + dp_trade(sums, step, 0)
        rest = rest + dp_trade(rest, step, 1)
    shares, tally = project(sums, dp_trade(sums, rounds - 1, 0), acts)
    keep, *sends = project_rest(rest, dp_trade(rest, rounds - 1, 1), tally, shares, turn(acts, first))
    shares = [feat_trade(sends[bits - 1], bits) for bits in range(feat - 1, 0, -1)]
    return scale([keep] + shares).T


def solution(mesh):
    return jax.shard_map(
        per_device,
        mesh=mesh,
        in_specs=(P("dp", "feat"), P("dp"), P("dp"), P("dp")),
        out_specs=P("dp", "feat"),
        check_vma=False,
    )
```

```python
import jax
import jax.numpy as jnp
from jax import lax
from jax.experimental import pallas as pl
from jax.experimental.pallas import tpu as pltpu
from jax.sharding import PartitionSpec as P

CAND_DEV = 1
PER_PROMPT = 16
LANES = 128
VMEM_LIMIT = 32 * 1024 * 1024

epsilon = 1e-06

VMEM = pl.BlockSpec(memory_space=pltpu.VMEM)
HBM = pl.BlockSpec(memory_space=pltpu.HBM)


def in_hbm(value):
    return pltpu.with_memory_space_constraint(value, pltpu.HBM)


def in_vmem(value):
    return pltpu.with_memory_space_constraint(value, pltpu.VMEM)


def member_kernel(counts_ref, cand_hbm, labels_hbm, member_ref, tally_ref, cand_ref, labels_ref, sems):
    classes, rows = member_ref.shape
    cands = classes // 2
    prompts = labels_ref.shape[1]
    copies = [
        pltpu.make_async_copy(source, target, sems.at[place])
        for place, (source, target) in enumerate(
            ((cand_hbm, cand_ref), (labels_hbm, labels_ref))
        )
    ]
    for copy in copies:
        copy.start()
    prompt_ids = lax.broadcasted_iota(jnp.int32, (prompts, rows), 0)
    prompt_of = lax.broadcasted_iota(jnp.int32, (prompts, rows), 1) // PER_PROMPT
    spread = jnp.where(prompt_ids == prompt_of, 1.0, 0.0).astype(jnp.bfloat16)
    wanted = lax.broadcasted_iota(jnp.int32, (classes, rows), 0)
    row_prompt = lax.broadcasted_iota(jnp.int32, (1, rows), 1) // PER_PROMPT
    for copy in copies:
        copy.wait()
    labels = jnp.broadcast_to(labels_ref[...].astype(jnp.float32), (8, prompts))
    row_class = jnp.dot(labels.astype(jnp.bfloat16), spread, preferred_element_type=jnp.float32)[:1]
    slot = jnp.where(row_class == 1.0, cand_ref[...], cand_ref[...] + cands)
    slot = jnp.where(row_prompt < counts_ref[0], slot, -1)
    member = jnp.where(wanted == slot, 1.0, 0.0)
    member_ref[...] = member.astype(jnp.bfloat16)
    tally = jnp.sum(member, axis=1, keepdims=True)
    tally_ref[...] = jnp.broadcast_to(tally, (classes, LANES))


def membership(cand_index, labels, counts, classes, width):
    rows, prompts = cand_index.shape[0], labels.shape[0]
    return pl.pallas_call(
        member_kernel,
        out_shape=(
            jax.ShapeDtypeStruct((classes, rows), jnp.bfloat16),
            jax.ShapeDtypeStruct((classes, LANES), jnp.float32),
        ),
        in_specs=[pl.BlockSpec(memory_space=pltpu.SMEM)] + [HBM] * 2,
        out_specs=(VMEM,) * 2,
        scratch_shapes=[
            pltpu.VMEM((1, rows), jnp.int32),
            pltpu.VMEM((1, prompts), jnp.int32),
            pltpu.SemaphoreType.DMA((2,)),
        ],
        cost_estimate=pl.CostEstimate(flops=800 * rows * width, bytes_accessed=0, transcendentals=0),
        compiler_params=pltpu.CompilerParams(vmem_limit_bytes=VMEM_LIMIT),
        name="membership",
    )(counts, in_hbm(cand_index.reshape(1, rows)), in_hbm(labels.reshape(1, prompts)))


def first_kernel(member_ref, tally_ref, acts_ref, sums_ref):
    first = sums_ref.shape[1] - LANES
    sums_ref[:, :first] = jnp.dot(
        member_ref[...], acts_ref[:, :first], preferred_element_type=jnp.float32
    )
    sums_ref[:, first:] = tally_ref[...]


def first_sums(member, tally, acts, first):
    return pl.pallas_call(
        first_kernel,
        out_shape=jax.ShapeDtypeStruct((member.shape[0], first + LANES), jnp.float32),
        in_specs=[VMEM] * 3,
        out_specs=VMEM,
        compiler_params=pltpu.CompilerParams(vmem_limit_bytes=VMEM_LIMIT),
        name="first_sums",
    )(in_vmem(member), in_vmem(tally), acts)


def rest_kernel(member_ref, acts_ref, sums_ref):
    first = acts_ref.shape[1] - sums_ref.shape[1]
    sums_ref[...] = jnp.dot(
        member_ref[...], acts_ref[:, first:], preferred_element_type=jnp.float32
    )


def rest_sums(member, acts, first):
    return pl.pallas_call(
        rest_kernel,
        out_shape=jax.ShapeDtypeStruct((member.shape[0], acts.shape[1] - first), jnp.float32),
        in_specs=[VMEM] * 2,
        out_specs=VMEM,
        compiler_params=pltpu.CompilerParams(vmem_limit_bytes=VMEM_LIMIT),
        name="rest_sums",
    )(in_vmem(member), acts)


def directions(total, tally):
    cands = total.shape[0] // 2
    harmful_mean = total[:cands] / tally[:cands]
    harmless_mean = total[cands:] / tally[cands:]
    raw_dir = (harmful_mean - harmless_mean).astype(jnp.bfloat16)
    return raw_dir, jnp.sum(jnp.square(raw_dir.astype(jnp.float32)), axis=1, keepdims=True)


def project_kernel(mine_ref, other_ref, acts_ref, shares_ref, tally_ref):
    rows = acts_ref.shape[0]
    first = mine_ref.shape[1] - LANES
    total = mine_ref[...] + other_ref[...]
    tally = jnp.maximum(total[:, first:], 1.0)
    tally_ref[...] = tally
    raw_dir, squares = directions(total[:, :first], tally[:, :1])
    shares_ref[:, :rows] = lax.dot_general(
        raw_dir, acts_ref[:, :first], (((1,), (1,)), ((), ())), preferred_element_type=jnp.float32
    )
    shares_ref[:, rows:] = jnp.broadcast_to(squares, (squares.shape[0], LANES))


def project(mine, other, acts):
    rows = acts.shape[0]
    classes = mine.shape[0]
    return pl.pallas_call(
        project_kernel,
        out_shape=(
            jax.ShapeDtypeStruct((classes // 2, rows + LANES), jnp.float32),
            jax.ShapeDtypeStruct((classes, LANES), jnp.float32),
        ),
        in_specs=[VMEM] * 3,
        out_specs=(VMEM,) * 2,
        compiler_params=pltpu.CompilerParams(vmem_limit_bytes=VMEM_LIMIT),
        name="project",
    )(mine, other, acts)


def turn_kernel(acts_ref, turned_ref):
    first = acts_ref.shape[1] - turned_ref.shape[0]
    turned_ref[...] = acts_ref[:, first:].T


def turn(acts, first):
    rows, width = acts.shape
    return pl.pallas_call(
        turn_kernel,
        out_shape=pltpu.VMEM((width - first, rows), acts.dtype),
        in_specs=[VMEM],
        out_specs=VMEM,
        compiler_params=pltpu.CompilerParams(vmem_limit_bytes=VMEM_LIMIT),
        name="turn",
    )(acts)


def project_rest_kernel(mine_ref, other_ref, tally_ref, shares_ref, turned_ref, keep_ref, *send_refs):
    rows = turned_ref.shape[1]
    cands = mine_ref.shape[0] // 2
    parts = len(send_refs) + 1
    part = cands // parts
    place = lax.axis_index("feat")
    raw_dir, squares = directions(mine_ref[...] + other_ref[...], tally_ref[:, :1])
    plain = jnp.dot(raw_dir, turned_ref[...], preferred_element_type=jnp.float32)
    plain = plain + shares_ref[:, :rows]
    squares = squares + shares_ref[:, rows:]
    for step, out_ref in enumerate((keep_ref,) + send_refs):
        for value, columns in ((plain, slice(0, rows)), (squares, slice(rows, rows + LANES))):
            chosen = value[:part]
            for block in range(1, parts):
                mine = place == block ^ step
                chosen = jnp.where(mine, value[block * part : (block + 1) * part], chosen)
            out_ref[:, columns] = chosen


def project_rest(mine, other, tally, shares, turned):
    rows = turned.shape[1]
    parts = lax.axis_size("feat")
    part = jax.ShapeDtypeStruct((mine.shape[0] // 2 // parts, rows + LANES), jnp.float32)
    return pl.pallas_call(
        project_rest_kernel,
        out_shape=(part,) * parts,
        in_specs=[VMEM] * 5,
        out_specs=(VMEM,) * parts,
        compiler_params=pltpu.CompilerParams(vmem_limit_bytes=VMEM_LIMIT),
        name="project_rest",
    )(mine, other, tally, shares, in_vmem(turned))


def scale_kernel(*refs):
    *share_refs, scores_ref = refs
    rows = scores_ref.shape[1]
    total = share_refs[0][...]
    for ref in share_refs[1:]:
        total = total + ref[...]
    inv_norm = lax.rsqrt(total[:, rows : rows + 1] + epsilon).astype(jnp.bfloat16)
    scores_ref[...] = total[:, :rows] * inv_norm.astype(jnp.float32)


def scale(shares):
    part, columns = shares[0].shape
    return pl.pallas_call(
        scale_kernel,
        out_shape=jax.ShapeDtypeStruct((part, columns - LANES), jnp.float32),
        in_specs=[VMEM] * len(shares),
        out_specs=VMEM,
        compiler_params=pltpu.CompilerParams(vmem_limit_bytes=VMEM_LIMIT),
        name="scale",
    )(*shares)


def dp_trade(value, step, half):
    dp, feat = lax.axis_size("dp"), lax.axis_size("feat")
    count = dp.bit_length() - 1
    up = list(range(count))
    even = (up, up[:1] + up[:0:-1])[half]
    odd = (up[::-1], up[1:2] + up[:1] + up[2:])[half]
    pairs = []
    for d in range(dp):
        for f in range(feat):
            bit = 1 << (odd if f % 2 else even)[step]
            pairs.append((d * feat + f, (d ^ bit) * feat + f))
    return lax.ppermute(value, ("dp", "feat"), pairs)


def feat_trade(value, bits):
    return lax.ppermute(value, "feat", [(f, f ^ bits) for f in range(lax.axis_size("feat"))])


def per_device(activations, cand_index, labels, counts):
    dp, feat = lax.axis_size("dp"), lax.axis_size("feat")
    first = activations.shape[1] // 2
    classes = 2 * CAND_DEV * dp
    acts = in_vmem(activations)
    member, tally = membership(cand_index, labels, counts, classes, activations.shape[1])
    sums = first_sums(member, tally, acts, first)
    rest = rest_sums(member, acts, first)
    rounds = dp.bit_length() - 1
    for step in range(rounds - 1):
        sums = sums + dp_trade(sums, step, 0)
        rest = rest + dp_trade(rest, step, 1)
    shares, tally = project(sums, dp_trade(sums, rounds - 1, 0), acts)
    keep, *sends = project_rest(rest, dp_trade(rest, rounds - 1, 1), tally, shares, turn(acts, first))
    shares = [feat_trade(sends[bits - 1], bits) for bits in range(feat - 1, 0, -1)]
    return scale([keep] + shares).T


def solution(mesh):
    return jax.shard_map(
        per_device,
        mesh=mesh,
        in_specs=(P("dp", "feat"), P("dp"), P("dp"), P("dp")),
        out_specs=P("dp", "feat"),
        check_vma=False,
    )
```

```python
import jax
import jax.numpy as jnp
from jax import lax
from jax.experimental import pallas as pl
from jax.experimental.pallas import tpu as pltpu
from jax.sharding import PartitionSpec as P

CAND_DEV = 1
PER_PROMPT = 16
LANES = 128
VMEM_LIMIT = 32 * 1024 * 1024

epsilon = 1e-06

VMEM = pl.BlockSpec(memory_space=pltpu.VMEM)
HBM = pl.BlockSpec(memory_space=pltpu.HBM)


def in_hbm(value):
    return pltpu.with_memory_space_constraint(value, pltpu.HBM)


def in_vmem(value):
    return pltpu.with_memory_space_constraint(value, pltpu.VMEM)


def member_kernel(counts_ref, cand_hbm, labels_hbm, member_ref, tally_ref, cand_ref, labels_ref, sems):
    classes, rows = member_ref.shape
    cands = classes // 2
    prompts = labels_ref.shape[1]
    copies = [
        pltpu.make_async_copy(source, target, sems.at[place])
        for place, (source, target) in enumerate(
            ((cand_hbm, cand_ref), (labels_hbm, labels_ref))
        )
    ]
    for copy in copies:
        copy.start()
    prompt_ids = lax.broadcasted_iota(jnp.int32, (prompts, rows), 0)
    prompt_of = lax.broadcasted_iota(jnp.int32, (prompts, rows), 1) // PER_PROMPT
    spread = jnp.where(prompt_ids == prompt_of, 1.0, 0.0).astype(jnp.bfloat16)
    wanted = lax.broadcasted_iota(jnp.int32, (classes, rows), 0)
    row_prompt = lax.broadcasted_iota(jnp.int32, (1, rows), 1) // PER_PROMPT
    for copy in copies:
        copy.wait()
    labels = jnp.broadcast_to(labels_ref[...].astype(jnp.float32), (8, prompts))
    row_class = jnp.dot(labels.astype(jnp.bfloat16), spread, preferred_element_type=jnp.float32)[:1]
    slot = jnp.where(row_class == 1.0, cand_ref[...], cand_ref[...] + cands)
    slot = jnp.where(row_prompt < counts_ref[0], slot, -1)
    member = jnp.where(wanted == slot, 1.0, 0.0)
    member_ref[...] = member.astype(jnp.bfloat16)
    tally = jnp.sum(member, axis=1, keepdims=True)
    tally_ref[...] = jnp.broadcast_to(tally, (classes, LANES))


def membership(cand_index, labels, counts, classes, width):
    rows, prompts = cand_index.shape[0], labels.shape[0]
    return pl.pallas_call(
        member_kernel,
        out_shape=(
            jax.ShapeDtypeStruct((classes, rows), jnp.bfloat16),
            jax.ShapeDtypeStruct((classes, LANES), jnp.float32),
        ),
        in_specs=[pl.BlockSpec(memory_space=pltpu.SMEM)] + [HBM] * 2,
        out_specs=(VMEM,) * 2,
        scratch_shapes=[
            pltpu.VMEM((1, rows), jnp.int32),
            pltpu.VMEM((1, prompts), jnp.int32),
            pltpu.SemaphoreType.DMA((2,)),
        ],
        cost_estimate=pl.CostEstimate(flops=800 * rows * width, bytes_accessed=0, transcendentals=0),
        compiler_params=pltpu.CompilerParams(vmem_limit_bytes=VMEM_LIMIT),
        name="membership",
    )(counts, in_hbm(cand_index.reshape(1, rows)), in_hbm(labels.reshape(1, prompts)))


def first_kernel(member_ref, tally_ref, acts_ref, sums_ref):
    first = sums_ref.shape[1] - LANES
    sums_ref[:, :first] = jnp.dot(
        member_ref[...], acts_ref[:, :first], preferred_element_type=jnp.float32
    )
    sums_ref[:, first:] = tally_ref[...]


def first_sums(member, tally, acts, first):
    return pl.pallas_call(
        first_kernel,
        out_shape=jax.ShapeDtypeStruct((member.shape[0], first + LANES), jnp.float32),
        in_specs=[VMEM] * 3,
        out_specs=VMEM,
        compiler_params=pltpu.CompilerParams(vmem_limit_bytes=VMEM_LIMIT),
        name="first_sums",
    )(in_vmem(member), in_vmem(tally), acts)


def rest_kernel(member_ref, acts_ref, sums_ref):
    first = acts_ref.shape[1] - sums_ref.shape[1]
    sums_ref[...] = jnp.dot(
        member_ref[...], acts_ref[:, first:], preferred_element_type=jnp.float32
    )


def rest_sums(member, acts, first):
    return pl.pallas_call(
        rest_kernel,
        out_shape=jax.ShapeDtypeStruct((member.shape[0], acts.shape[1] - first), jnp.float32),
        in_specs=[VMEM] * 2,
        out_specs=VMEM,
        compiler_params=pltpu.CompilerParams(vmem_limit_bytes=VMEM_LIMIT),
        name="rest_sums",
    )(in_vmem(member), acts)


def directions(total, tally):
    cands = total.shape[0] // 2
    harmful_mean = total[:cands] / tally[:cands]
    harmless_mean = total[cands:] / tally[cands:]
    raw_dir = (harmful_mean - harmless_mean).astype(jnp.bfloat16)
    return raw_dir, jnp.sum(jnp.square(raw_dir.astype(jnp.float32)), axis=1, keepdims=True)


def project_kernel(mine_ref, other_ref, acts_ref, shares_ref, tally_ref):
    rows = acts_ref.shape[0]
    first = mine_ref.shape[1] - LANES
    total = mine_ref[...] + other_ref[...]
    tally = jnp.maximum(total[:, first:], 1.0)
    tally_ref[...] = tally
    raw_dir, squares = directions(total[:, :first], tally[:, :1])
    shares_ref[:, :rows] = lax.dot_general(
        raw_dir, acts_ref[:, :first], (((1,), (1,)), ((), ())), preferred_element_type=jnp.float32
    )
    shares_ref[:, rows:] = jnp.broadcast_to(squares, (squares.shape[0], LANES))


def project(mine, other, acts):
    rows = acts.shape[0]
    classes = mine.shape[0]
    return pl.pallas_call(
        project_kernel,
        out_shape=(
            jax.ShapeDtypeStruct((classes // 2, rows + LANES), jnp.float32),
            jax.ShapeDtypeStruct((classes, LANES), jnp.float32),
        ),
        in_specs=[VMEM] * 3,
        out_specs=(VMEM,) * 2,
        compiler_params=pltpu.CompilerParams(vmem_limit_bytes=VMEM_LIMIT),
        name="project",
    )(mine, other, acts)


def turn_kernel(acts_ref, turned_ref):
    first = acts_ref.shape[1] - turned_ref.shape[0]
    turned_ref[...] = acts_ref[:, first:].T


def turn(acts, first):
    rows, width = acts.shape
    return pl.pallas_call(
        turn_kernel,
        out_shape=pltpu.VMEM((width - first, rows), acts.dtype),
        in_specs=[VMEM],
        out_specs=VMEM,
        compiler_params=pltpu.CompilerParams(vmem_limit_bytes=VMEM_LIMIT),
        name="turn",
    )(acts)


def project_rest_kernel(mine_ref, other_ref, tally_ref, shares_ref, turned_ref, keep_ref, *send_refs):
    rows = turned_ref.shape[1]
    cands = mine_ref.shape[0] // 2
    parts = len(send_refs) + 1
    part = cands // parts
    place = lax.axis_index("feat")
    plain, squares = shares_ref[:, :rows], shares_ref[:, rows:]
    tall = turned_ref.shape[0] // 4
    for piece in range(4):
        here = slice(piece * tall, (piece + 1) * tall)
        raw_dir, piece_squares = directions(mine_ref[:, here] + other_ref[:, here], tally_ref[:, :1])
        plain = plain + jnp.dot(raw_dir, turned_ref[here, :], preferred_element_type=jnp.float32)
        squares = squares + piece_squares
    for step, out_ref in enumerate((keep_ref,) + send_refs):
        for value, columns in ((plain, slice(0, rows)), (squares, slice(rows, rows + LANES))):
            chosen = value[:part]
            for block in range(1, parts):
                mine = place == block ^ step
                chosen = jnp.where(mine, value[block * part : (block + 1) * part], chosen)
            out_ref[:, columns] = chosen


def project_rest(mine, other, tally, shares, turned):
    rows = turned.shape[1]
    parts = lax.axis_size("feat")
    part = jax.ShapeDtypeStruct((mine.shape[0] // 2 // parts, rows + LANES), jnp.float32)
    return pl.pallas_call(
        project_rest_kernel,
        out_shape=(part,) * parts,
        in_specs=[VMEM] * 5,
        out_specs=(VMEM,) * parts,
        compiler_params=pltpu.CompilerParams(vmem_limit_bytes=VMEM_LIMIT),
        name="project_rest",
    )(mine, other, tally, shares, in_vmem(turned))


def scale_kernel(*refs):
    *share_refs, scores_ref = refs
    rows = scores_ref.shape[1]
    total = share_refs[0][...]
    for ref in share_refs[1:]:
        total = total + ref[...]
    inv_norm = lax.rsqrt(total[:, rows : rows + 1] + epsilon).astype(jnp.bfloat16)
    scores_ref[...] = total[:, :rows] * inv_norm.astype(jnp.float32)


def scale(shares):
    part, columns = shares[0].shape
    return pl.pallas_call(
        scale_kernel,
        out_shape=jax.ShapeDtypeStruct((part, columns - LANES), jnp.float32),
        in_specs=[VMEM] * len(shares),
        out_specs=VMEM,
        compiler_params=pltpu.CompilerParams(vmem_limit_bytes=VMEM_LIMIT),
        name="scale",
    )(*shares)


def dp_trade(value, step, half):
    dp, feat = lax.axis_size("dp"), lax.axis_size("feat")
    count = dp.bit_length() - 1
    up = list(range(count))
    even = (up, up[:1] + up[:0:-1])[half]
    odd = up[-1:] + up[:-1]
    pairs = []
    for d in range(dp):
        for f in range(feat):
            bit = 1 << (odd if f % 2 else even)[step]
            pairs.append((d * feat + f, (d ^ bit) * feat + f))
    return lax.ppermute(value, ("dp", "feat"), pairs)


def feat_trade(value, bits):
    return lax.ppermute(value, "feat", [(f, f ^ bits) for f in range(lax.axis_size("feat"))])


def per_device(activations, cand_index, labels, counts):
    dp, feat = lax.axis_size("dp"), lax.axis_size("feat")
    first = activations.shape[1] // 2
    classes = 2 * CAND_DEV * dp
    acts = in_vmem(activations)
    member, tally = membership(cand_index, labels, counts, classes, activations.shape[1])
    sums = first_sums(member, tally, acts, first)
    rest = rest_sums(member, acts, first)
    rounds = dp.bit_length() - 1
    for step in range(rounds - 1):
        sums = sums + dp_trade(sums, step, 0)
        rest = rest + dp_trade(rest, step, 1)
    shares, tally = project(sums, dp_trade(sums, rounds - 1, 0), acts)
    keep, *sends = project_rest(rest, dp_trade(rest, rounds - 1, 1), tally, shares, turn(acts, first))
    shares = [feat_trade(sends[bits - 1], bits) for bits in range(feat - 1, 0, -1)]
    return scale([keep] + shares).T


def solution(mesh):
    return jax.shard_map(
        per_device,
        mesh=mesh,
        in_specs=(P("dp", "feat"), P("dp"), P("dp"), P("dp")),
        out_specs=P("dp", "feat"),
        check_vma=False,
    )
```
